512 devices in a mesh: row: 32 (over x, z), col: 16 (over y, core).
Axes of the slice: x: 4, y: 8, z: 8, core: 2. Of those that a mesh axis runs over, the one named last changes fastest.
Arguments:
- trail_points: bfloat16 [2048, 2560], P('row', 'col'), may hold values from -7 to 7
- block_points: bfloat16 [1024, 2560], P('col', 'row'), may hold values from -7 to 7
- cand_points: bfloat16 [2048, 2560], P('row', 'col'), may hold values from -7 to 7
- trail_factor: float32 [2048, 4096], P('row', 'col'), may hold values from -0.0359375 to 0.0359375
- block_factor: float32 [1024, 4096], P('row', 'col'), may hold values from -0.015625 to 0.015625
- cand_solved: float32 [4096, 2048], P('col', 'row'), may hold values from -0.0328125 to 0.0328125
- noise: float32 [1024], P('row'), may hold values from 1 to 4
Outputs:
- diag_factor: float32 [1024, 1024], P('col')
- panel: float32 [1024, 2048], P('col', 'row')
- cand_solve: float32 [1024, 2048], P('col', 'row')
The draws below stay inside these ranges and needn't reach their ends.
All inputs are finite; a program needn't handle non-finite values.
Results may differ from the reference program's by a relative error of at most 0.0012.
Values may be sent and summed in bfloat16 or wider, within the bound.
No kernel may reach another device: no remote copies, remote signals or barrier semaphores. Data moves between devices by JAX's collectives and lax.ppermute only.
A program may use at most 64 MiB of HBM per device.

```python
import math
import jax
import jax.numpy as jnp
from jax import lax

D = 2560
B = 1024
P_SIZE = 4096
ROWS = 2048
CANDS = 2048


def point_cloud(key, count, tag):
    key_mean = jax.random.fold_in(key, 101)
    key_centers = jax.random.fold_in(key, 103)
    key_own = jax.random.fold_in(key, tag)
    key_ids = jax.random.fold_in(key_own, 1)
    key_weights = jax.random.fold_in(key_own, 2)
    key_noise = jax.random.fold_in(key_own, 3)
    center_count = 16
    mean = 0.5 * jax.random.truncated_normal(key_mean, -3.0, 3.0, (D,), jnp.float32)
    centers = jax.random.truncated_normal(key_centers, -3.0, 3.0, (center_count, D), jnp.float32)
    jitter = jax.random.truncated_normal(key_noise, -3.0, 3.0, (count, D), jnp.float32)
    picks = jax.random.randint(key_ids, (count, 2), 0, center_count)
    weights = jax.random.uniform(key_weights, (count, 2), jnp.float32, 0.2, 0.8)
    mixed = weights[:, 0:1] * centers[picks[:, 0]] + weights[:, 1:2] * centers[picks[:, 1]]
    deviation = mixed + 0.2 * jitter
    values = jnp.clip(mean[None, :] + deviation, -7.0, 7.0)
    return values.astype(jnp.bfloat16)


def draw_trail_points(key, part):
    return point_cloud(key, ROWS, 211)


def draw_block_points(key, part):
    return point_cloud(key, B, 223)


def draw_cand_points(key, part):
    return point_cloud(key, CANDS, 227)


def factor_base(key):
    base = jax.random.uniform(jax.random.fold_in(key, 301), (B, P_SIZE), jnp.float32, -0.866, 0.866) * P_SIZE ** (-0.5)
    return base


def draw_block_factor(key, part):
    return factor_base(key).astype(jnp.float32)


def draw_trail_factor(key, part):
    base = factor_base(key)
    picks = jax.random.randint(jax.random.fold_in(key, 311), (ROWS,), 0, B)
    extra = jax.random.uniform(jax.random.fold_in(key, 313), (ROWS, P_SIZE), jnp.float32, -0.5, 0.5) * P_SIZE ** (-0.5)
    return (1.8 * base[picks] + extra).astype(jnp.float32)


def draw_cand_solved(key, part):
    base = factor_base(key)
    picks = jax.random.randint(jax.random.fold_in(key, 317), (CANDS,), 0, B)
    extra = jax.random.uniform(jax.random.fold_in(key, 319), (P_SIZE, CANDS), jnp.float32, -0.5, 0.5) * P_SIZE ** (-0.5)
    return (1.6 * base[picks].T + extra).astype(jnp.float32)


def levels(rng, extent, cuts, smallest, high):
    gain, own = 1.0, jax.random.fold_in(rng, 6)
    for dim, parts in cuts:
        draws = jnp.exp(jax.random.uniform(jax.random.fold_in(own, dim), (parts,), jnp.float32, smallest / len(cuts), high / len(cuts)))
        gain = gain * jnp.repeat(draws, extent[dim] // parts).reshape([-1 if axis == dim else 1 for axis in range(len(extent))])
    return gain


def setup_inputs(seed: int = 0) -> dict:
    streams_of = jax.random.split(jax.random.key(seed), 8)
    trail_points = draw_trail_points(jax.random.fold_in(streams_of[7], 71), 0)
    block_points = draw_block_points(jax.random.fold_in(streams_of[7], 71), 0)
    cand_points = draw_cand_points(jax.random.fold_in(streams_of[7], 71), 0)
    trail_factor = draw_trail_factor(jax.random.fold_in(streams_of[7], 71), 0)
    block_factor = draw_block_factor(jax.random.fold_in(streams_of[7], 71), 0)
    cand_solved = draw_cand_solved(jax.random.fold_in(streams_of[7], 71), 0)
    noise = jnp.clip(jnp.exp(math.log(4.0) - 1.3862944 * jax.random.uniform(streams_of[6], (B,), jnp.float32) ** levels(streams_of[6], (B,), ((0, 32),), -0.2, 0.2)), 1.0, 4.0)
    return dict(trail_points=trail_points, block_points=block_points, cand_points=cand_points, trail_factor=trail_factor, block_factor=block_factor, cand_solved=cand_solved, noise=noise)


def matern(left_points, right_points):
    inner_products = jnp.dot(left_points.astype(jnp.float32), right_points.T.astype(jnp.float32), preferred_element_type=jnp.float32)
    left_norms = lax.optimization_barrier(jnp.sum(jnp.square(left_points.astype(jnp.float32)), axis=1))
    right_norms = lax.optimization_barrier(jnp.sum(jnp.square(right_points.astype(jnp.float32)), axis=1))
    squared = jnp.maximum(left_norms[:, None] + right_norms[None, :] - 2.0 * inner_products, 0.0)
    scaled = jnp.sqrt(5.0 * squared / D)
    return (1.0 + scaled + scaled * scaled / 3.0) * jnp.exp(-scaled)

def reference(trail_points, block_points, cand_points, trail_factor, block_factor, cand_solved, noise):
    highest = lax.Precision.HIGHEST
    block_cov = matern(block_points, block_points) + jnp.diag(noise) - jnp.dot(block_factor.astype(jnp.float32), block_factor.T.astype(jnp.float32), precision=highest, preferred_element_type=jnp.float32)
    diag_factor = jnp.linalg.cholesky(block_cov)
    below_cov = matern(trail_points, block_points) - jnp.dot(trail_factor.astype(jnp.float32), block_factor.T.astype(jnp.float32), precision=highest, preferred_element_type=jnp.float32)
    panel = lax.linalg.triangular_solve(diag_factor, below_cov.T, left_side=True, lower=True)
    cand_cov = matern(block_points, cand_points) - jnp.dot(block_factor.astype(jnp.float32), cand_solved.astype(jnp.float32), precision=highest, preferred_element_type=jnp.float32)
    cand_solve = lax.linalg.triangular_solve(diag_factor, cand_cov, left_side=True, lower=True)
    return (diag_factor, panel, cand_solve)
```

```python
import jax
import jax.numpy as jnp
from jax import lax
from jax.experimental import pallas as pl
from jax.experimental.pallas import tpu as pltpu
from jax.sharding import PartitionSpec as P

D = 2560

N = 1024
BLK = 128
f32, bf16 = jnp.float32, jnp.bfloat16


def split(x):
    high = x.astype(bf16)
    return high, (x - high.astype(f32)).astype(bf16)


def mm(a, b, bt=False):
    dims = (((1,), (1 if bt else 0,)), ((), ()))
    return lax.dot_general(a, b, dims, preferred_element_type=f32)


def dot3(a, b, bt=False):
    ah, al = split(a)
    bh, bl = split(b)
    return mm(ah, bh, bt) + (mm(ah, bl, bt) + mm(al, bh, bt))


def rows_of(x):
    return [jnp.broadcast_to(x[k : k + 1, :], (8, BLK)) for k in range(8)]


def lane(x, j):
    return jnp.broadcast_to(x[:, j : j + 1], (8, BLK))


def factor_inverse(D, store):
    sub = lax.broadcasted_iota(jnp.int32, (8, BLK), 0)
    ln = lax.broadcasted_iota(jnp.int32, (8, BLK), 1)
    E = [jnp.where(sub + 8 * v == ln, 1.0, 0.0).astype(f32) for v in range(16)]
    for g in range(16):
        R, RE = rows_of(D[g]), rows_of(E[g])
        G = {}
        for i in range(8):
            for l in range(i, 8):
                G[i, l] = lane(R[i], 8 * g + l)
        M = {v: [lane(D[v], 8 * g + k) for k in range(8)] for v in range(g + 1, 16)}
        inv, F = [], {}
        for i in range(8):
            r = 1.0 / G[i, i]
            inv.append(r)
            if i < 7:
                nxt = G[i, i + 1] * G[i, i + 1]
            for l in range(i + 1, 8):
                F[l, i] = G[i, l] * r
            for l in range(i + 1, 8):
                for m in range(l, 8):
                    if l == i + 1 and m == l:
                        G[l, m] = G[l, m] - nxt * r
                    else:
                        G[l, m] = G[l, m] - F[l, i] * G[i, m]
            for l in range(i + 1, 8):
                RE[l] = RE[l] - F[l, i] * RE[i]
                R[l] = R[l] - F[l, i] * R[i]
        out = RE[0] * lax.rsqrt(G[0, 0])
        for i in range(1, 8):
            out = jnp.where(sub == i, RE[i] * lax.rsqrt(G[i, i]), out)
        store(g, out)
        if g == 15:
            break
        V, VE = [None] * 8, [None] * 8
        for i in range(7, -1, -1):
            a, b = R[i] * inv[i], RE[i] * inv[i]
            for l in range(i + 1, 8):
                a = a - F[l, i] * V[l]
                b = b - F[l, i] * VE[l]
            V[i], VE[i] = a, b
        for v in range(g + 1, 16):
            d, e = D[v], E[v]
            for k in range(8):
                d = d - M[v][k] * V[k]
                e = e - M[v][k] * VE[k]
            D[v], E[v] = d, e


def kernel(c_ref, a_ref, rhs_ref, diag_ref, w_ref, t, linv, uph, upl):
    c = c_ref[0]
    width = N + BLK

    def fill(i, _):
        r = pl.multiple_of(i * BLK, BLK)
        t[pl.ds(r, BLK), :N] = a_ref[pl.ds(r, BLK), :]
        t[pl.ds(r, BLK), N:] = rhs_ref[pl.ds(r, BLK), :]
        return 0

    lax.fori_loop(0, 8, fill, 0)

    def step(kb, _):
        base = pl.multiple_of(kb * BLK, BLK)
        D = [t[pl.ds(pl.multiple_of(base + 8 * v, 8), 8), pl.ds(base, BLK)] for v in range(16)]

        def store(g, rows):
            linv[8 * g : 8 * g + 8, :] = rows

        factor_inverse(D, store)
        lh, ll = split(linv[...])
        mine = pl.multiple_of(c * 64, 64)
        lc = t[pl.ds(mine, 64), pl.ds(base, BLK)]
        ch, cl = split(lc)
        low = mm(ch, lh, True) + (mm(cl, lh, True) + mm(ch, ll, True))
        ri = lax.broadcasted_iota(jnp.int32, (64, BLK), 0) + mine
        ci = lax.broadcasted_iota(jnp.int32, (64, BLK), 1) + base
        diag_ref[:, pl.ds(base, BLK)] = jnp.where(ri >= ci, low, 0.0)
        for n0 in range(0, width, 384):
            x = t[pl.ds(base, BLK), n0 : n0 + 384]
            xh, xl = split(x)
            u = mm(lh, xh) + (mm(ll, xh) + mm(lh, xl))
            uh, ul = split(u)
            uph[:, n0 : n0 + 384] = uh
            upl[:, n0 : n0 + 384] = ul
            if n0 + 384 == width:
                t[pl.ds(base, BLK), N:] = u[:, 256:]

        def update(jb, _):
            r = pl.multiple_of(jb * BLK, BLK)
            ah, al = split(t[pl.ds(r, BLK), pl.ds(base, BLK)])
            lp = mm(ah, lh, True) + (mm(al, lh, True) + mm(ah, ll, True))
            ph, pl_ = split(lp)
            for n0 in range(0, width, 384):
                uh, ul = uph[:, n0 : n0 + 384], upl[:, n0 : n0 + 384]
                t[pl.ds(r, BLK), n0 : n0 + 384] -= mm(ph, uh) + (mm(ph, ul) + mm(pl_, uh))
            return 0

        lax.fori_loop(kb + 1, 8, update, 0)
        return 0

    lax.fori_loop(0, 8, step, 0)
    w_ref[...] = t[pl.ds(pl.multiple_of(c * 64, 64), 64), N:]


def chol_solve(c, a, rhs):
    return pl.pallas_call(
        kernel,
        out_shape=(jax.ShapeDtypeStruct((64, N), f32), jax.ShapeDtypeStruct((64, BLK), f32)),
        in_specs=[pl.BlockSpec(memory_space=pltpu.SMEM), pl.BlockSpec(memory_space=pltpu.VMEM), pl.BlockSpec(memory_space=pltpu.VMEM)],
        out_specs=(pl.BlockSpec(memory_space=pltpu.VMEM), pl.BlockSpec(memory_space=pltpu.VMEM)),
        scratch_shapes=[
            pltpu.VMEM((N, N + BLK), f32),
            pltpu.VMEM((BLK, BLK), f32),
            pltpu.VMEM((BLK, N + BLK), bf16),
            pltpu.VMEM((BLK, N + BLK), bf16),
        ],
        compiler_params=pltpu.CompilerParams(vmem_limit_bytes=40 * 1024 * 1024),
        cost_estimate=pl.CostEstimate(flops=3 * 10**9, bytes_accessed=5 * 10**6, transcendentals=0),
    )(c, a, rhs)


def spread(value, axis, count):
    copies = jnp.broadcast_to(value[None], (count,) + value.shape)
    return lax.all_to_all(lax.optimization_barrier(copies), axis, 0, 0)


def sum_scatter(value, axis, count):
    rows = value.shape[0] // count
    parts = lax.all_to_all(value.reshape((count, rows) + value.shape[1:]), axis, 0, 0)
    return jnp.sum(parts, axis=0)


def matern(inner, left_norms, right_norms):
    squared = jnp.maximum(left_norms[:, None] + right_norms[None, :] - 2.0 * inner, 0.0)
    scaled = jnp.sqrt(5.0 * squared / D)
    return (1.0 + scaled + scaled * scaled / 3.0) * jnp.exp(-scaled)


def norms(points):
    return jnp.sum(jnp.square(points.astype(f32)), axis=0)


def times(a, b, dims):
    high, low = split(b)
    one = lax.dot_general(a, high, (dims, ((), ())), preferred_element_type=f32)
    return one + lax.dot_general(a, low, (dims, ((), ())), preferred_element_type=f32)


def body(trail_points, block_points, cand_points, trail_factor, block_factor, cand_solved, noise):
    rows, cols = 32, 16
    row_index = lax.axis_index("row")
    col_index = lax.axis_index("col")
    block_t = block_points.T
    same, other = [], []
    for r in range(rows):
        for c in range(cols):
            half = r % 2
            same.append((r * cols + c, (2 * c + half) * cols + r // 2))
            other.append((r * cols + c, (2 * c + 1 - half) * cols + r // 2))
    odd = row_index % 2
    halves = (block_t[:, :32], block_t[:, 32:])
    mine = lax.ppermute(jnp.where(odd == 0, halves[0], halves[1]), ("row", "col"), same)
    theirs = lax.ppermute(jnp.where(odd == 0, halves[1], halves[0]), ("row", "col"), other)
    local_t = jnp.where(
        odd == 0, jnp.concatenate([mine, theirs], axis=0), jnp.concatenate([theirs, mine], axis=0)
    )
    all_factor = spread(block_factor.astype(bf16), "row", rows).reshape(N, -1)
    own_t = spread(block_t, "row", rows).reshape(D, -1)
    points_t = lax.all_gather(
        jnp.concatenate([trail_points.T, cand_points.T, local_t], axis=1), "col", axis=0, tiled=True
    )
    inner = lax.dot_general(own_t, points_t, (((0,), (0,)), ((), ())), preferred_element_type=f32)
    kernel_tile = matern(inner, norms(own_t), norms(points_t))

    diag_part = times(all_factor, block_factor, ((1,), (1,)))
    rhs_part = jnp.concatenate(
        [
            times(all_factor, trail_factor, ((1,), (1,))),
            times(all_factor, cand_solved, ((1,), (0,))),
        ],
        axis=1,
    )
    column_ids = col_index * 64 + jnp.arange(64, dtype=jnp.int32)
    row_ids = row_index * 32 + jnp.arange(32, dtype=jnp.int32)
    on_diagonal = column_ids[:, None] == row_ids[None, :]
    diag_tile = kernel_tile[:, 128:] - sum_scatter(diag_part, "col", cols)
    diag_tile = diag_tile + jnp.where(on_diagonal, noise[None, :], 0.0)
    diag_rows = spread(diag_tile, "row", rows).transpose(1, 0, 2).reshape(64, N)
    diag_rows, rhs_part = lax.optimization_barrier((diag_rows, rhs_part))
    whole = lax.all_gather(diag_rows, "col", axis=0, tiled=True)
    rhs_tile = kernel_tile[:, :128] - sum_scatter(rhs_part, "col", cols)
    rhs = lax.all_gather(rhs_tile, "col", axis=0, tiled=True)
    diag_out, solved = chol_solve(col_index.reshape(1).astype(jnp.int32), whole, rhs)
    return (diag_out, solved[:, :64], solved[:, 64:])


def solution(mesh):
    return jax.shard_map(
        body,
        mesh=mesh,
        in_specs=(
            P("row", "col"),
            P("col", "row"),
            P("row", "col"),
            P("row", "col"),
            P("row", "col"),
            P("col", "row"),
            P("row"),
        ),
        out_specs=(P("col", None), P("col", "row"), P("col", "row")),
        check_vma=False,
    )
```

```python
import jax
import jax.numpy as jnp
from jax import lax
from jax.experimental import pallas as pl
from jax.experimental.pallas import tpu as pltpu
from jax.sharding import PartitionSpec as P

D = 2560
PAD = 128

N = 1024
BLK = 128
f32, bf16 = jnp.float32, jnp.bfloat16


def split(x):
    high = x.astype(bf16)
    return high, (x - high.astype(f32)).astype(bf16)


def mm(a, b, bt=False):
    dims = (((1,), (1 if bt else 0,)), ((), ()))
    return lax.dot_general(a, b, dims, preferred_element_type=f32)


def dot3(a, b, bt=False):
    ah, al = split(a)
    bh, bl = split(b)
    return mm(ah, bh, bt) + (mm(ah, bl, bt) + mm(al, bh, bt))


def rows_of(x):
    return [jnp.broadcast_to(x[k : k + 1, :], (8, BLK)) for k in range(8)]


def lane(x, j):
    return jnp.broadcast_to(x[:, j : j + 1], (8, BLK))


def factor_inverse(D, store):
    sub = lax.broadcasted_iota(jnp.int32, (8, BLK), 0)
    ln = lax.broadcasted_iota(jnp.int32, (8, BLK), 1)
    E = [jnp.where(sub + 8 * v == ln, 1.0, 0.0).astype(f32) for v in range(16)]
    for g in range(16):
        R, RE = rows_of(D[g]), rows_of(E[g])
        G = {}
        for i in range(8):
            for l in range(i, 8):
                G[i, l] = lane(R[i], 8 * g + l)
        M = {v: [lane(D[v], 8 * g + k) for k in range(8)] for v in range(g + 1, 16)}
        inv, F = [], {}
        for i in range(8):
            r = 1.0 / G[i, i]
            inv.append(r)
            if i < 7:
                nxt = G[i, i + 1] * G[i, i + 1]
            for l in range(i + 1, 8):
                F[l, i] = G[i, l] * r
            for l in range(i + 1, 8):
                for m in range(l, 8):
                    if l == i + 1 and m == l:
                        G[l, m] = G[l, m] - nxt * r
                    else:
                        G[l, m] = G[l, m] - F[l, i] * G[i, m]
            for l in range(i + 1, 8):
                RE[l] = RE[l] - F[l, i] * RE[i]
                R[l] = R[l] - F[l, i] * R[i]
        out = RE[0] * lax.rsqrt(G[0, 0])
        for i in range(1, 8):
            out = jnp.where(sub == i, RE[i] * lax.rsqrt(G[i, i]), out)
        store(g, out)
        if g == 15:
            break
        V, VE = [None] * 8, [None] * 8
        for i in range(7, -1, -1):
            a, b = R[i] * inv[i], RE[i] * inv[i]
            for l in range(i + 1, 8):
                a = a - F[l, i] * V[l]
                b = b - F[l, i] * VE[l]
            V[i], VE[i] = a, b
        for v in range(g + 1, 16):
            d, e = D[v], E[v]
            for k in range(8):
                d = d - M[v][k] * V[k]
                e = e - M[v][k] * VE[k]
            D[v], E[v] = d, e


def kernel(c_ref, a_ref, rhs_ref, diag_ref, w_ref, t, linv, uph, upl):
    c = c_ref[0]
    width = N + BLK

    for block in range(16):
        slab = a_ref[64 * block : 64 * block + 64, :]
        if block:
            slab = pltpu.roll(slab, 64 * block, 1)
        t[64 * block : 64 * block + 64, :N] = slab

    def fill(i, _):
        r = pl.multiple_of(i * BLK, BLK)
        t[pl.ds(r, BLK), N:] = rhs_ref[pl.ds(r, BLK), :]
        return 0

    lax.fori_loop(0, 8, fill, 0)

    def step(kb, _):
        base = pl.multiple_of(kb * BLK, BLK)
        D = [t[pl.ds(pl.multiple_of(base + 8 * v, 8), 8), pl.ds(base, BLK)] for v in range(16)]

        def store(g, rows):
            linv[8 * g : 8 * g + 8, :] = rows

        factor_inverse(D, store)
        lh, ll = split(linv[...])
        mine = pl.multiple_of(c * 64, 64)
        lc = t[pl.ds(mine, 64), pl.ds(base, BLK)]
        ch, cl = split(lc)
        low = mm(ch, lh, True) + (mm(cl, lh, True) + mm(ch, ll, True))
        ri = lax.broadcasted_iota(jnp.int32, (64, BLK), 0) + mine
        ci = lax.broadcasted_iota(jnp.int32, (64, BLK), 1) + base
        diag_ref[:, pl.ds(base, BLK)] = jnp.where(ri >= ci, low, 0.0)
        for n0 in range(0, width, 384):
            x = t[pl.ds(base, BLK), n0 : n0 + 384]
            xh, xl = split(x)
            u = mm(lh, xh) + (mm(ll, xh) + mm(lh, xl))
            uh, ul = split(u)
            uph[:, n0 : n0 + 384] = uh
            upl[:, n0 : n0 + 384] = ul
            if n0 + 384 == width:
                t[pl.ds(base, BLK), N:] = u[:, 256:]

        def update(jb, _):
            r = pl.multiple_of(jb * BLK, BLK)
            ah, al = split(t[pl.ds(r, BLK), pl.ds(base, BLK)])
            lp = mm(ah, lh, True) + (mm(al, lh, True) + mm(ah, ll, True))
            ph, pl_ = split(lp)
            for n0 in range(0, width, 384):
                uh, ul = uph[:, n0 : n0 + 384], upl[:, n0 : n0 + 384]
                t[pl.ds(r, BLK), n0 : n0 + 384] -= mm(ph, uh) + (mm(ph, ul) + mm(pl_, uh))
            return 0

        lax.fori_loop(kb + 1, 8, update, 0)
        return 0

    lax.fori_loop(0, 8, step, 0)
    w_ref[...] = t[pl.ds(pl.multiple_of(c * 64, 64), 64), N:]


def chol_solve(c, a, rhs):
    return pl.pallas_call(
        kernel,
        out_shape=(jax.ShapeDtypeStruct((64, N), f32), jax.ShapeDtypeStruct((64, BLK), f32)),
        in_specs=[pl.BlockSpec(memory_space=pltpu.SMEM), pl.BlockSpec(memory_space=pltpu.VMEM), pl.BlockSpec(memory_space=pltpu.VMEM)],
        out_specs=(pl.BlockSpec(memory_space=pltpu.VMEM), pl.BlockSpec(memory_space=pltpu.VMEM)),
        scratch_shapes=[
            pltpu.VMEM((N, N + BLK), f32),
            pltpu.VMEM((BLK, BLK), f32),
            pltpu.VMEM((BLK, N + BLK), bf16),
            pltpu.VMEM((BLK, N + BLK), bf16),
        ],
        compiler_params=pltpu.CompilerParams(vmem_limit_bytes=40 * 1024 * 1024),
        cost_estimate=pl.CostEstimate(flops=3 * 10**9, bytes_accessed=5 * 10**6, transcendentals=0),
    )(c, a, rhs)


def spread(value, axis, count):
    copies = jnp.broadcast_to(value[None], (count,) + value.shape)
    return lax.all_to_all(lax.optimization_barrier(copies), axis, 0, 0)


def matern(inner, left_norms, right_norms):
    squared = jnp.maximum(left_norms[:, None] + right_norms[None, :] - 2.0 * inner, 0.0)
    scaled = jnp.sqrt(5.0 * squared / D)
    return (1.0 + scaled + scaled * scaled / 3.0) * jnp.exp(-scaled)


def norms(points):
    return jnp.sum(jnp.square(points.astype(f32)), axis=0)


def times(a, b, dims):
    return lax.dot_general(a, b.astype(bf16), (dims, ((), ())), preferred_element_type=f32)


def body(trail_points, block_points, cand_points, trail_factor, block_factor, cand_solved, noise):
    rows, cols = 32, 16
    row_index = lax.axis_index("row")
    col_index = lax.axis_index("col")
    odd = row_index % 2
    distance = row_index // 2
    pad = jnp.zeros((trail_points.shape[1], PAD), bf16)
    points_t = lax.all_gather(
        jnp.concatenate([trail_points.T, cand_points.T, pad], axis=1), "col", axis=0, tiled=True
    )
    own_t = spread(block_points.T, "row", rows).reshape(D, -1)
    hop = []
    for r in range(rows):
        for c in range(cols):
            hop.append((r * cols + (c + r // 2) % cols, r * cols + c))
    half = jnp.where(odd == 0, own_t[:, :32], own_t[:, 32:])
    partner_t = lax.ppermute(half, ("row", "col"), hop)
    factor = spread(block_factor.astype(bf16), "row", rows).reshape(cols, 64, -1)
    turned = lax.dynamic_slice(
        jnp.concatenate([factor, factor], axis=0),
        (distance, 32 * odd, 0),
        (cols, 32, factor.shape[2]),
    )
    diag_part = lax.dot_general(
        factor, turned, (((2,), (2,)), ((0,), (0,))), preferred_element_type=f32
    )
    diag_sum = jnp.sum(lax.all_to_all(diag_part, "col", 0, 0), axis=0)
    own_norms = norms(own_t)
    inner = lax.dot_general(own_t, partner_t, (((0,), (0,)), ((), ())), preferred_element_type=f32)
    diag_tile = matern(inner, own_norms, norms(partner_t)) - diag_sum
    sent = jnp.concatenate([diag_tile, noise[None, :], jnp.zeros((7, 32), f32)], axis=0)
    got = spread(sent, "row", rows)
    own_noise = lax.dynamic_slice(got[:, 64, :], (2 * col_index, 0), (2, 32)).reshape(64)
    diag_rows = got[:, :64, :].transpose(1, 0, 2).reshape(64, N)
    place = jnp.arange(64, dtype=jnp.int32)[:, None] == jnp.arange(N, dtype=jnp.int32)[None, :]
    diag_rows = diag_rows + jnp.where(place, own_noise[:, None], 0.0)
    diag_rows, factor = lax.optimization_barrier((diag_rows, factor))
    whole = lax.all_gather(diag_rows, "col", axis=0, tiled=True)

    factor = factor.reshape(N, -1)
    rhs_part = jnp.concatenate(
        [times(factor, trail_factor, ((1,), (1,))), times(factor, cand_solved, ((1,), (0,)))], axis=1
    )
    rhs_parts = lax.all_to_all(rhs_part.astype(bf16).reshape(cols, 64, BLK), "col", 0, 0)
    rhs_sum = jnp.sum(rhs_parts.astype(f32), axis=0)
    points_t = points_t[:, :BLK]
    inner = lax.dot_general(own_t, points_t, (((0,), (0,)), ((), ())), preferred_element_type=f32)
    rhs_tile = matern(inner, own_norms, norms(points_t)) - rhs_sum
    rhs = lax.all_gather(rhs_tile, "col", axis=0, tiled=True)
    diag_out, solved = chol_solve(col_index.reshape(1).astype(jnp.int32), whole, rhs)
    return (diag_out, solved[:, :64], solved[:, 64:])


def solution(mesh):
    return jax.shard_map(
        body,
        mesh=mesh,
        in_specs=(
            P("row", "col"),
            P("col", "row"),
            P("row", "col"),
            P("row", "col"),
            P("row", "col"),
            P("col", "row"),
            P("row"),
        ),
        out_specs=(P("col", None), P("col", "row"), P("col", "row")),
        check_vma=False,
    )
```

```python
import functools

import jax
import jax.numpy as jnp
from jax import lax
from jax.experimental import pallas as pl
from jax.experimental.pallas import tpu as pltpu
from jax.sharding import PartitionSpec as P

D = 2560
PAD = 128

N = 1024
BLK = 128
f32, bf16 = jnp.float32, jnp.bfloat16


def split(x):
    high = x.astype(bf16)
    return high, (x - high.astype(f32)).astype(bf16)


def mm(a, b, bt=False):
    dims = (((1,), (1 if bt else 0,)), ((), ()))
    return lax.dot_general(a, b, dims, preferred_element_type=f32)


def left(x):
    high, low = split(x)
    return jnp.concatenate([high, high, low], axis=1)


def right(x, axis=1):
    high, low = split(x)
    return jnp.concatenate([high, low, high], axis=axis)


def rows_of(x):
    return [jnp.broadcast_to(x[k : k + 1, :], (8, BLK)) for k in range(8)]


def lane(x, j):
    return jnp.broadcast_to(x[:, j : j + 1], (8, BLK))


def recip(x):
    r = pl.reciprocal(x, approx=True)
    return r * (2.0 - x * r)


def tree(terms):
    while len(terms) > 1:
        terms = [sum(terms[i : i + 2][1:], terms[i]) for i in range(0, len(terms), 2)]
    return terms[0]


def factor_inverse(D, store):
    sub = lax.broadcasted_iota(jnp.int32, (8, BLK), 0)
    ln = lax.broadcasted_iota(jnp.int32, (8, BLK), 1)
    E = [jnp.where(sub + 8 * v == ln, 1.0, 0.0).astype(f32) for v in range(16)]
    for g in range(16):
        R, RE = rows_of(D[g]), rows_of(E[g])
        G = {}
        for i in range(8):
            for l in range(i, 8):
                G[i, l] = lane(R[i], 8 * g + l)
        M = {v: [lane(D[v], 8 * g + k) for k in range(8)] for v in range(g + 1, 16)}
        X = list(M[g + 1]) if g < 15 else None
        C, Z, ZE, out = {}, [None] * 8, [None] * 8, None
        for i in range(0, 8, 2):
            p, q, s = G[i, i], G[i, i + 1], G[i + 1, i + 1]
            det = p * s - q * q
            inv = 1.0 / det
            first, last = {}, {}
            for l in range(i + 2, 8):
                first[l] = s * G[i, l] - q * G[i + 1, l]
                last[l] = p * G[i + 1, l] - q * G[i, l]
            for l in range(i + 2, 8):
                for m in range(l, 8):
                    G[l, m] = G[l, m] - (G[i, m] * first[l] + G[i + 1, m] * last[l]) * inv
            pinv, sinv, qinv = p * inv, s * inv, q * inv
            Z[i], Z[i + 1] = sinv * R[i] - qinv * R[i + 1], pinv * R[i + 1] - qinv * R[i]
            ZE[i], ZE[i + 1] = sinv * RE[i] - qinv * RE[i + 1], pinv * RE[i + 1] - qinv * RE[i]
            for l in range(i + 2, 8):
                C[l, i], C[l, i + 1] = first[l] * inv, last[l] * inv
                R[l] = R[l] - (C[l, i] * R[i] + C[l, i + 1] * R[i + 1])
                RE[l] = RE[l] - (C[l, i] * RE[i] + C[l, i + 1] * RE[i + 1])
                if X:
                    X[l] = X[l] - (C[l, i] * X[i] + C[l, i + 1] * X[i + 1])
            ratio = 1.0 / p
            even = RE[i] * lax.rsqrt(p)
            odd = (RE[i + 1] - (q * ratio) * RE[i]) * lax.rsqrt(det * ratio)
            out = even if out is None else jnp.where(sub == i, even, out)
            out = jnp.where(sub == i + 1, odd, out)
        store(g, out)
        if g == 15:
            break
        d = D[g + 1] - tree([X[k] * Z[k] for k in range(6)])
        D[g + 1] = d - (X[6] * Z[6] + X[7] * Z[7])
        E[g + 1] = E[g + 1] - tree([X[k] * ZE[k] for k in range(8)])
        V, VE = [None] * 8, [None] * 8
        for i in range(7, -1, -1):
            low = i + 2 - i % 2
            V[i], VE[i] = Z[i], ZE[i]
            if low < 8:
                V[i] = V[i] - tree([C[l, i] * V[l] for l in range(low, 8)])
                VE[i] = VE[i] - tree([C[l, i] * VE[l] for l in range(low, 8)])
        for v in range(g + 2, 16):
            D[v] = D[v] - tree([M[v][k] * V[k] for k in range(8)])
            E[v] = E[v] - tree([M[v][k] * VE[k] for k in range(8)])


def eliminate(i, t, rt, pa, pb, inverse, solved):
    start = (i + 1) * BLK
    if start == N:
        return
    panel = mm(left(t[start:, i * BLK : start]), inverse, True)
    pa[start:, :] = left(panel)
    pb[start:, :] = right(panel)
    rt[start:, :] -= mm(pa[start:, :], solved)
    first = start
    while first < N:
        wide = 256 if (N - first) % 256 == 0 else 128
        t[first:, first : first + wide] -= mm(pa[first:, :], pb[first : first + wide, :], True)
        first += wide


def kernel(c_ref, a_ref, rhs_ref, diag_ref, panel_ref, cand_ref, t, rt, linv, pa, pb, sems):
    copies = []
    for k in range(8):
        rows = pl.ds(k * BLK, BLK)
        edge = N - k * BLK
        pieces = [(0, k * BLK, edge)] + ([(edge, 0, k * BLK)] if k else [])
        for source, target, width in pieces:
            copies.append(
                pltpu.make_async_copy(
                    a_ref.at[rows, pl.ds(source, width)],
                    t.at[rows, pl.ds(target, width)],
                    sems.at[len(copies)],
                )
            )
            copies[-1].start()
    mine = pl.multiple_of(c_ref[0] * 64, 64)
    rt[...] = rhs_ref[...]
    copies[0].wait()

    def step(kb, _):
        base = pl.multiple_of(kb * BLK, BLK)
        D = [t[pl.ds(pl.multiple_of(base + 8 * v, 8), 8), pl.ds(base, BLK)] for v in range(16)]

        def store(g, rows):
            linv[8 * g : 8 * g + 8, :] = rows

        factor_inverse(D, store)

        @pl.when(kb == 0)
        def _():
            for copy in copies[1:]:
                copy.wait()

        inverse = right(linv[...])
        low = mm(left(t[pl.ds(mine, 64), pl.ds(base, BLK)]), inverse, True)
        ri = lax.broadcasted_iota(jnp.int32, (64, BLK), 0) + mine
        ci = lax.broadcasted_iota(jnp.int32, (64, BLK), 1) + base
        diag_ref[:, pl.ds(base, BLK)] = jnp.where(ri >= ci, low, 0.0)
        solved = mm(left(linv[...]), right(rt[pl.ds(base, BLK), :], 0))
        rt[pl.ds(base, BLK), :] = solved
        solved = right(solved, 0)
        for i in range(8):
            pl.when(kb == i)(functools.partial(eliminate, i, t, rt, pa, pb, inverse, solved))
        return 0

    lax.fori_loop(0, 8, step, 0)
    panel_ref[...] = rt[pl.ds(mine, 64), :64]
    cand_ref[...] = rt[pl.ds(mine, 64), 64:]


def chol_solve(c, a, rhs):
    return pl.pallas_call(
        kernel,
        out_shape=(
            jax.ShapeDtypeStruct((64, N), f32),
            jax.ShapeDtypeStruct((64, 64), f32),
            jax.ShapeDtypeStruct((64, 64), f32),
        ),
        in_specs=[
            pl.BlockSpec(memory_space=pltpu.SMEM),
            pl.BlockSpec(memory_space=pl.ANY),
            pl.BlockSpec(memory_space=pltpu.VMEM),
        ],
        out_specs=(pl.BlockSpec(memory_space=pltpu.VMEM),) * 3,
        scratch_shapes=[
            pltpu.VMEM((N, N), f32),
            pltpu.VMEM((N, BLK), f32),
            pltpu.VMEM((BLK, BLK), f32),
            pltpu.VMEM((N, 3 * BLK), bf16),
            pltpu.VMEM((N, 3 * BLK), bf16),
            pltpu.SemaphoreType.DMA((15,)),
        ],
        compiler_params=pltpu.CompilerParams(vmem_limit_bytes=60 * 1024 * 1024),
        cost_estimate=pl.CostEstimate(flops=3 * 10**9, bytes_accessed=5 * 10**6, transcendentals=0),
    )(c, a, rhs)


SMALL = pltpu.CompilerParams(vmem_limit_bytes=8 * 1024 * 1024)


def slab_kernel(c_ref, tiles_ref, out_ref):
    swap = c_ref[0] % 2
    place = lax.broadcasted_iota(jnp.int32, (16, BLK), 1) // 32
    for d in range(8):
        four = []
        for side in range(2):
            for half in range(2):
                four.append(tiles_ref[4 * d + 2 * (side + swap - 2 * side * swap) + half])
        for q in range(4):
            piece = four[0] if q == 0 else pltpu.roll(four[0], BLK - 32 * q, 1)
            for k in range(1, 4):
                turn = (32 * (k - q)) % BLK
                piece = jnp.where(place == k, pltpu.roll(four[k], turn, 1) if turn else four[k], piece)
            out_ref[16 * q : 16 * q + 16, BLK * d : BLK * d + BLK] = piece


def row_slab(c, tiles):
    return pl.pallas_call(
        slab_kernel,
        out_shape=jax.ShapeDtypeStruct((64, N), f32),
        in_specs=[pl.BlockSpec(memory_space=pltpu.SMEM), pl.BlockSpec(memory_space=pltpu.VMEM)],
        out_specs=pl.BlockSpec(memory_space=pltpu.VMEM),
        compiler_params=SMALL,
    )(c, tiles)


def product_kernel(place_ref, packed_ref, out_ref):
    distance, side, half = place_ref[0], place_ref[1], place_ref[2]
    lanes = lax.broadcasted_iota(jnp.int32, (16, BLK), 1) // 32
    for c in range(16):
        other = 2 * ((c // 2 + distance) % 8) + (side + c) % 2
        total = None
        for part in range(2):
            at = slice(32 * part, 32 * part + 32)
            left_rows = jnp.concatenate([packed_ref[2 * c, at, :], packed_ref[2 * c + 1, at, :]], axis=0)
            right_rows = packed_ref[2 * other + half, at, :]
            one = mm(left_rows, jnp.concatenate([right_rows] * 4, axis=0), True)
            total = one if total is None else total + one
        piece = total[:16]
        for q in range(1, 4):
            piece = jnp.where(lanes == q, total[16 * q : 16 * q + 16], piece)
        out_ref[c] = piece


def tile_products(place, packed):
    return pl.pallas_call(
        product_kernel,
        out_shape=jax.ShapeDtypeStruct((16, 16, BLK), f32),
        in_specs=[pl.BlockSpec(memory_space=pltpu.SMEM), pl.BlockSpec(memory_space=pltpu.VMEM)],
        out_specs=pl.BlockSpec(memory_space=pltpu.VMEM),
        compiler_params=SMALL,
    )(place, packed)


def finish_kernel(parts_ref, tile_ref, out_ref):
    total = tree([parts_ref[c] for c in range(16)])
    result = tile_ref[...] - total
    for r in range(32):
        out_ref[r] = result


def finish_tile(parts, tile):
    return pl.pallas_call(
        finish_kernel,
        out_shape=jax.ShapeDtypeStruct((32, 16, BLK), f32),
        in_specs=[pl.BlockSpec(memory_space=pltpu.VMEM), pl.BlockSpec(memory_space=pltpu.VMEM)],
        out_specs=pl.BlockSpec(memory_space=pltpu.VMEM),
        compiler_params=SMALL,
    )(parts, tile)


def spread(value, axis, count):
    copies = jnp.broadcast_to(value[None], (count,) + value.shape)
    return lax.all_to_all(lax.optimization_barrier(copies), axis, 0, 0)


def matern(inner, left_norms, right_norms):
    squared = jnp.maximum(left_norms[:, None] + right_norms[None, :] - 2.0 * inner, 0.0)
    scaled = jnp.sqrt(5.0 * squared / D)
    return (1.0 + scaled + scaled * scaled / 3.0) * jnp.exp(-scaled)


def norms(points):
    return jnp.sum(jnp.square(points.astype(f32)), axis=0)


def times(a, b, dims):
    return lax.dot_general(a, b.astype(bf16), (dims, ((), ())), preferred_element_type=f32)


def body(trail_points, block_points, cand_points, trail_factor, block_factor, cand_solved, noise):
    rows, cols = 32, 16
    row_index = lax.axis_index("row")
    col_index = lax.axis_index("col")
    odd = row_index % 2
    side = row_index // 2 % 2
    distance = row_index // 4
    pad = jnp.zeros((trail_points.shape[1], PAD), bf16)
    points_t = lax.all_gather(
        jnp.concatenate([trail_points.T, cand_points.T, pad], axis=1), "col", axis=0, tiled=True
    )
    block_t = block_points.T
    flat = block_factor.astype(bf16)
    packed = jnp.concatenate(
        [flat[:, :BLK], flat[:, BLK:], jnp.concatenate([block_t[:40], block_t[40:]], axis=1)], axis=0
    )
    packed = spread(packed, "row", rows)
    settle = [((2 * c + h) * cols + c, h * cols + c) for c in range(cols) for h in range(2)]
    own_noise = lax.ppermute(noise, ("row", "col"), settle)
    hop = []
    for r in range(rows):
        for c in range(cols):
            partner = 2 * ((c // 2 + r // 4) % 8) + (r // 2 + c) % 2
            hop.append((r * cols + partner, r * cols + c))
    own = packed[:, 64:, :].reshape(D // 2, BLK)
    partner = lax.ppermute(own, ("row", "col"), hop)
    place = jnp.stack([distance, side, odd]).astype(jnp.int32)
    parts = lax.all_to_all(tile_products(place, packed), "col", 0, 0)
    own_norms = norms(own)
    own_norms = own_norms[:64] + own_norms[64:]
    partner_norms = norms(partner)
    partner_norms = partner_norms[:64] + partner_norms[64:]
    inner = lax.dot_general(own, partner, (((0,), (0,)), ((), ())), preferred_element_type=f32)
    tile = matern(inner[:64, :64] + inner[64:, 64:], own_norms, partner_norms)
    tile = jnp.where(odd == 0, tile[:, :32], tile[:, 32:])
    line = jnp.arange(64, dtype=jnp.int32)[:, None] - 32 * odd
    tile = tile + jnp.where(line == jnp.arange(32, dtype=jnp.int32)[None, :], own_noise[None, :], 0.0)
    tile = jnp.concatenate([tile[16 * q : 16 * q + 16] for q in range(4)], axis=1)
    sent = finish_tile(parts, lax.optimization_barrier(tile))
    diag_rows = row_slab(col_index.reshape(1), lax.all_to_all(sent, "row", 0, 0))
    diag_rows, packed = lax.optimization_barrier((diag_rows, packed))
    whole = lax.all_gather(diag_rows, "col", axis=0, tiled=True)

    factor = jnp.concatenate([packed[:, :32], packed[:, 32:64]], axis=2).reshape(N, -1)
    rhs_part = jnp.concatenate(
        [times(factor, trail_factor, ((1,), (1,))), times(factor, cand_solved, ((1,), (0,)))], axis=1
    )
    rhs_parts = lax.all_to_all(rhs_part.astype(bf16).reshape(cols, 64, BLK), "col", 0, 0)
    rhs_sum = jnp.sum(rhs_parts.astype(f32), axis=0)
    points_t = points_t[:, :BLK]
    own_t = jnp.stack([packed[:, 64:, :64], packed[:, 64:, 64:]], axis=1).reshape(D, -1)
    inner = lax.dot_general(own_t, points_t, (((0,), (0,)), ((), ())), preferred_element_type=f32)
    rhs_tile = matern(inner, own_norms, norms(points_t)) - rhs_sum
    rhs = lax.all_gather(rhs_tile, "col", axis=0, tiled=True)
    return chol_solve(col_index.reshape(1).astype(jnp.int32), whole, rhs)


def solution(mesh):
    return jax.shard_map(
        body,
        mesh=mesh,
        in_specs=(
            P("row", "col"),
            P("col", "row"),
            P("row", "col"),
            P("row", "col"),
            P("row", "col"),
            P("col", "row"),
            P("row"),
        ),
        out_specs=(P("col", None), P("col", "row"), P("col", "row")),
        check_vma=False,
    )
```

```python
import functools

import jax
import jax.numpy as jnp
from jax import lax
from jax.experimental import pallas as pl
from jax.experimental.pallas import tpu as pltpu
from jax.sharding import PartitionSpec as P

D = 2560
PAD = 128

N = 1024
BLK = 128
f32, bf16 = jnp.float32, jnp.bfloat16


def split(x):
    high = x.astype(bf16)
    return high, (x - high.astype(f32)).astype(bf16)


def mm(a, b, bt=False):
    dims = (((1,), (1 if bt else 0,)), ((), ()))
    return lax.dot_general(a, b, dims, preferred_element_type=f32)


def left(x):
    high, low = split(x)
    return jnp.concatenate([high, high, low], axis=1)


def right(x, axis=1):
    high, low = split(x)
    return jnp.concatenate([high, low, high], axis=axis)


def rows_of(x):
    return [jnp.broadcast_to(x[k : k + 1, :], (8, BLK)) for k in range(8)]


def lane(x, j):
    return jnp.broadcast_to(x[:, j : j + 1], (8, BLK))


def recip(x):
    r = pl.reciprocal(x, approx=True)
    return r * (2.0 - x * r)


def tree(terms):
    while len(terms) > 1:
        terms = [sum(terms[i : i + 2][1:], terms[i]) for i in range(0, len(terms), 2)]
    return terms[0]


def factor_inverse(D, store):
    sub = lax.broadcasted_iota(jnp.int32, (8, BLK), 0)
    ln = lax.broadcasted_iota(jnp.int32, (8, BLK), 1)
    E = [jnp.where(sub + 8 * v == ln, 1.0, 0.0).astype(f32) for v in range(16)]
    for g in range(16):
        R, RE = rows_of(D[g]), rows_of(E[g])
        G = {}
        for i in range(8):
            for l in range(i, 8):
                G[i, l] = lane(R[i], 8 * g + l)
        M = {v: [lane(D[v], 8 * g + k) for k in range(8)] for v in range(g + 1, 16)}
        X = list(M[g + 1]) if g < 15 else None
        C, Z, ZE, out = {}, [None] * 8, [None] * 8, None
        for i in range(0, 8, 2):
            p, q, s = G[i, i], G[i, i + 1], G[i + 1, i + 1]
            det = p * s - q * q
            inv = 1.0 / det
            first, last = {}, {}
            for l in range(i + 2, 8):
                first[l] = s * G[i, l] - q * G[i + 1, l]
                last[l] = p * G[i + 1, l] - q * G[i, l]
            for l in range(i + 2, 8):
                for m in range(l, 8):
                    G[l, m] = G[l, m] - (G[i, m] * first[l] + G[i + 1, m] * last[l]) * inv
            pinv, sinv, qinv = p * inv, s * inv, q * inv
            Z[i], Z[i + 1] = sinv * R[i] - qinv * R[i + 1], pinv * R[i + 1] - qinv * R[i]
            ZE[i], ZE[i + 1] = sinv * RE[i] - qinv * RE[i + 1], pinv * RE[i + 1] - qinv * RE[i]
            for l in range(i + 2, 8):
                C[l, i], C[l, i + 1] = first[l] * inv, last[l] * inv
                R[l] = R[l] - (C[l, i] * R[i] + C[l, i + 1] * R[i + 1])
                RE[l] = RE[l] - (C[l, i] * RE[i] + C[l, i + 1] * RE[i + 1])
                if X:
                    X[l] = X[l] - (C[l, i] * X[i] + C[l, i + 1] * X[i + 1])
            ratio = 1.0 / p
            even = RE[i] * lax.rsqrt(p)
            odd = (RE[i + 1] - (q * ratio) * RE[i]) * lax.rsqrt(det * ratio)
            out = even if out is None else jnp.where(sub == i, even, out)
            out = jnp.where(sub == i + 1, odd, out)
        store(g, out)
        if g == 15:
            break
        d = D[g + 1] - tree([X[k] * Z[k] for k in range(6)])
        D[g + 1] = d - (X[6] * Z[6] + X[7] * Z[7])
        E[g + 1] = E[g + 1] - tree([X[k] * ZE[k] for k in range(8)])
        V, VE = [None] * 8, [None] * 8
        for i in range(7, -1, -1):
            low = i + 2 - i % 2
            V[i], VE[i] = Z[i], ZE[i]
            if low < 8:
                V[i] = V[i] - tree([C[l, i] * V[l] for l in range(low, 8)])
                VE[i] = VE[i] - tree([C[l, i] * VE[l] for l in range(low, 8)])
        for v in range(g + 2, 16):
            D[v] = D[v] - tree([M[v][k] * V[k] for k in range(8)])
            E[v] = E[v] - tree([M[v][k] * VE[k] for k in range(8)])


def eliminate(i, t, rt, pa, pb, inverse, solved):
    start = (i + 1) * BLK
    if start == N:
        return
    panel = mm(left(t[start:, i * BLK : start]), inverse, True)
    pa[start:, :] = left(panel)
    pb[start:, :] = right(panel)
    rt[start:, :] -= mm(pa[start:, :], solved)
    first = start
    while first < N:
        wide = 256 if (N - first) % 256 == 0 else 128
        t[first:, first : first + wide] -= mm(pa[first:, :], pb[first : first + wide, :], True)
        first += wide


def kernel(c_ref, a_ref, rhs_ref, diag_ref, panel_ref, cand_ref, t, rt, linv, pa, pb, sems):
    copies = []
    for k in range(8):
        rows = pl.ds(k * BLK, BLK)
        edge = N - k * BLK
        pieces = [(0, k * BLK, edge)] + ([(edge, 0, k * BLK)] if k else [])
        for source, target, width in pieces:
            copies.append(
                pltpu.make_async_copy(
                    a_ref.at[rows, pl.ds(source, width)],
                    t.at[rows, pl.ds(target, width)],
                    sems.at[len(copies)],
                )
            )
            copies[-1].start()
    mine = pl.multiple_of(c_ref[0] * 64, 64)
    rt[...] = rhs_ref[...]
    copies[0].wait()

    def step(kb, _):
        base = pl.multiple_of(kb * BLK, BLK)
        D = [t[pl.ds(pl.multiple_of(base + 8 * v, 8), 8), pl.ds(base, BLK)] for v in range(16)]

        def store(g, rows):
            linv[8 * g : 8 * g + 8, :] = rows

        factor_inverse(D, store)

        @pl.when(kb == 0)
        def _():
            for copy in copies[1:]:
                copy.wait()

        inverse = right(linv[...])
        low = mm(left(t[pl.ds(mine, 64), pl.ds(base, BLK)]), inverse, True)
        ri = lax.broadcasted_iota(jnp.int32, (64, BLK), 0) + mine
        ci = lax.broadcasted_iota(jnp.int32, (64, BLK), 1) + base
        diag_ref[:, pl.ds(base, BLK)] = jnp.where(ri >= ci, low, 0.0)
        solved = mm(left(linv[...]), right(rt[pl.ds(base, BLK), :], 0))
        rt[pl.ds(base, BLK), :] = solved
        solved = right(solved, 0)
        for i in range(8):
            pl.when(kb == i)(functools.partial(eliminate, i, t, rt, pa, pb, inverse, solved))
        return 0

    lax.fori_loop(0, 8, step, 0)
    panel_ref[...] = rt[pl.ds(mine, 64), :64]
    cand_ref[...] = rt[pl.ds(mine, 64), 64:]


def chol_solve(c, a, rhs):
    return pl.pallas_call(
        kernel,
        out_shape=(
            jax.ShapeDtypeStruct((64, N), f32),
            jax.ShapeDtypeStruct((64, 64), f32),
            jax.ShapeDtypeStruct((64, 64), f32),
        ),
        in_specs=[
            pl.BlockSpec(memory_space=pltpu.SMEM),
            pl.BlockSpec(memory_space=pl.ANY),
            pl.BlockSpec(memory_space=pltpu.VMEM),
        ],
        out_specs=(pl.BlockSpec(memory_space=pltpu.VMEM),) * 3,
        scratch_shapes=[
            pltpu.VMEM((N, N), f32),
            pltpu.VMEM((N, BLK), f32),
            pltpu.VMEM((BLK, BLK), f32),
            pltpu.VMEM((N, 3 * BLK), bf16),
            pltpu.VMEM((N, 3 * BLK), bf16),
            pltpu.SemaphoreType.DMA((15,)),
        ],
        compiler_params=pltpu.CompilerParams(vmem_limit_bytes=60 * 1024 * 1024),
        cost_estimate=pl.CostEstimate(flops=3 * 10**9, bytes_accessed=5 * 10**6, transcendentals=0),
    )(c, a, rhs)


SMALL = pltpu.CompilerParams(vmem_limit_bytes=8 * 1024 * 1024)


def slab_kernel(c_ref, tiles_ref, out_ref):
    swap = c_ref[0] % 2
    place = lax.broadcasted_iota(jnp.int32, (16, BLK), 1) // 32
    for d in range(8):
        four = []
        for side in range(2):
            for half in range(2):
                four.append(tiles_ref[4 * d + 2 * (side + swap - 2 * side * swap) + half])
        for q in range(4):
            piece = four[0] if q == 0 else pltpu.roll(four[0], BLK - 32 * q, 1)
            for k in range(1, 4):
                turn = (32 * (k - q)) % BLK
                piece = jnp.where(place == k, pltpu.roll(four[k], turn, 1) if turn else four[k], piece)
            out_ref[16 * q : 16 * q + 16, BLK * d : BLK * d + BLK] = piece


def row_slab(c, tiles):
    return pl.pallas_call(
        slab_kernel,
        out_shape=jax.ShapeDtypeStruct((64, N), f32),
        in_specs=[pl.BlockSpec(memory_space=pltpu.SMEM), pl.BlockSpec(memory_space=pltpu.VMEM)],
        out_specs=pl.BlockSpec(memory_space=pltpu.VMEM),
        compiler_params=SMALL,
    )(c, tiles)


def product_kernel(place_ref, packed_ref, out_ref, half_ref):
    distance, side, half = place_ref[0], place_ref[1], place_ref[2]
    lanes = lax.broadcasted_iota(jnp.int32, (16, BLK), 1) // 32
    group = lax.broadcasted_iota(jnp.int32, (80, BLK), 1) // 32
    for r in range(0, 16, 2):
        upper, lower = (
            jnp.concatenate([packed_ref[k, 64:, :].astype(f32), packed_ref[k + 1, 64:, :].astype(f32)], axis=0)
            for k in (r, 16 + r)
        )
        whole = jnp.where(half == 0, upper, pltpu.roll(upper, 96, 1))
        other = jnp.where(half == 0, pltpu.roll(lower, 64, 1), pltpu.roll(lower, 32, 1))
        near = jnp.where(group == 0, whole, pltpu.roll(whole, 96, 1))
        far = jnp.where(group == 2, other, pltpu.roll(other, 96, 1))
        half_ref[40 * r : 40 * r + 80, :] = jnp.where(group < 2, near, far).astype(bf16)
    for c in range(16):
        other = 2 * ((c // 2 + distance) % 8) + (side + c) % 2
        total = None
        for part in range(2):
            at = slice(32 * part, 32 * part + 32)
            left_rows = jnp.concatenate([packed_ref[2 * c, at, :], packed_ref[2 * c + 1, at, :]], axis=0)
            right_rows = packed_ref[2 * other + half, at, :]
            one = mm(left_rows, jnp.concatenate([right_rows] * 4, axis=0), True)
            total = one if total is None else total + one
        piece = total[:16]
        for q in range(1, 4):
            piece = jnp.where(lanes == q, total[16 * q : 16 * q + 16], piece)
        out_ref[c] = piece


def tile_products(place, packed):
    return pl.pallas_call(
        product_kernel,
        out_shape=(
            jax.ShapeDtypeStruct((16, 16, BLK), f32),
            jax.ShapeDtypeStruct((D // 4, BLK), bf16),
        ),
        in_specs=[pl.BlockSpec(memory_space=pltpu.SMEM), pl.BlockSpec(memory_space=pltpu.VMEM)],
        out_specs=(pl.BlockSpec(memory_space=pltpu.VMEM),) * 2,
        compiler_params=SMALL,
    )(place, packed)


def finish_kernel(parts_ref, tile_ref, out_ref):
    total = tree([parts_ref[c] for c in range(16)])
    result = tile_ref[...] - total
    for r in range(32):
        out_ref[r] = result


def finish_tile(parts, tile):
    return pl.pallas_call(
        finish_kernel,
        out_shape=jax.ShapeDtypeStruct((32, 16, BLK), f32),
        in_specs=[pl.BlockSpec(memory_space=pltpu.VMEM), pl.BlockSpec(memory_space=pltpu.VMEM)],
        out_specs=pl.BlockSpec(memory_space=pltpu.VMEM),
        compiler_params=SMALL,
    )(parts, tile)


def spread(value, axis, count):
    copies = jnp.broadcast_to(value[None], (count,) + value.shape)
    return lax.all_to_all(lax.optimization_barrier(copies), axis, 0, 0)


def matern(inner, left_norms, right_norms):
    squared = jnp.maximum(left_norms[:, None] + right_norms[None, :] - 2.0 * inner, 0.0)
    scaled = jnp.sqrt(5.0 * squared / D)
    return (1.0 + scaled + scaled * scaled / 3.0) * jnp.exp(-scaled)


def norms(points):
    return jnp.sum(jnp.square(points.astype(f32)), axis=0)


def times(a, b, dims):
    return lax.dot_general(a, b.astype(bf16), (dims, ((), ())), preferred_element_type=f32)


def body(trail_points, block_points, cand_points, trail_factor, block_factor, cand_solved, noise):
    rows, cols = 32, 16
    row_index = lax.axis_index("row")
    col_index = lax.axis_index("col")
    odd = row_index % 2
    side = row_index // 2 % 2
    distance = row_index // 4
    pad = jnp.zeros((trail_points.shape[1], PAD), bf16)
    points_t = lax.all_gather(
        jnp.concatenate([trail_points.T, cand_points.T, pad], axis=1), "col", axis=0, tiled=True
    )
    block_t = block_points.T
    flat = block_factor.astype(bf16)
    packed = jnp.concatenate(
        [flat[:, :BLK], flat[:, BLK:], jnp.concatenate([block_t[:40], block_t[40:]], axis=1)], axis=0
    )
    packed = spread(packed, "row", rows)
    settle = [((2 * c + h) * cols + c, h * cols + c) for c in range(cols) for h in range(2)]
    own_noise = lax.ppermute(noise, ("row", "col"), settle)
    hop = []
    for r in range(rows):
        for c in range(cols):
            partner = 2 * ((c // 2 + r // 4) % 8) + (r // 2 + c) % 2
            hop.append((r * cols + partner, r * cols + c))
    place = jnp.stack([distance, side, odd]).astype(jnp.int32)
    products, half = tile_products(place, packed)
    partner = lax.ppermute(half, ("row", "col"), hop)
    parts = lax.all_to_all(products, "col", 0, 0)
    own = packed[:, 64:, :].reshape(D // 2, BLK)
    own_norms = norms(own)
    own_norms = own_norms[:64] + own_norms[64:]
    partner_norms = jnp.sum(norms(partner).reshape(4, 32), axis=0)
    ends = (((0,), (0,)), ((), ()))
    near = lax.dot_general(own[: D // 4], partner, ends, preferred_element_type=f32)
    far = lax.dot_general(own[D // 4 :], partner, ends, preferred_element_type=f32)
    inner = (near[:64, :32] + near[64:, 32:64]) + (far[:64, 64:96] + far[64:, 96:])
    tile = matern(inner, own_norms, partner_norms)
    line = jnp.arange(64, dtype=jnp.int32)[:, None] - 32 * odd
    tile = tile + jnp.where(line == jnp.arange(32, dtype=jnp.int32)[None, :], own_noise[None, :], 0.0)
    tile = jnp.concatenate([tile[16 * q : 16 * q + 16] for q in range(4)], axis=1)
    sent = finish_tile(parts, lax.optimization_barrier(tile))
    diag_rows = row_slab(col_index.reshape(1), lax.all_to_all(sent, "row", 0, 0))
    diag_rows, packed = lax.optimization_barrier((diag_rows, packed))
    whole = lax.all_gather(diag_rows, "col", axis=0, tiled=True)

    factor = jnp.concatenate([packed[:, :32], packed[:, 32:64]], axis=2).reshape(N, -1)
    rhs_part = jnp.concatenate(
        [times(factor, trail_factor, ((1,), (1,))), times(factor, cand_solved, ((1,), (0,)))], axis=1
    )
    rhs_parts = lax.all_to_all(rhs_part.astype(bf16).reshape(cols, 64, BLK), "col", 0, 0)
    rhs_sum = jnp.sum(rhs_parts.astype(f32), axis=0)
    points_t = points_t[:, :BLK]
    own_t = jnp.stack([packed[:, 64:, :64], packed[:, 64:, 64:]], axis=1).reshape(D, -1)
    inner = lax.dot_general(own_t, points_t, (((0,), (0,)), ((), ())), preferred_element_type=f32)
    rhs_tile = matern(inner, own_norms, norms(points_t)) - rhs_sum
    rhs = lax.all_gather(rhs_tile, "col", axis=0, tiled=True)
    return chol_solve(col_index.reshape(1).astype(jnp.int32), whole, rhs)


def solution(mesh):
    return jax.shard_map(
        body,
        mesh=mesh,
        in_specs=(
            P("row", "col"),
            P("col", "row"),
            P("row", "col"),
            P("row", "col"),
            P("row", "col"),
            P("col", "row"),
            P("row"),
        ),
        out_specs=(P("col", None), P("col", "row"), P("col", "row")),
        check_vma=False,
    )
```

```python
import jax
import jax.numpy as jnp
from jax import lax
from jax.experimental import pallas as pl
from jax.experimental.pallas import tpu as pltpu
from jax.sharding import PartitionSpec as P

D = 2560
PAD = 128

N = 1024
BLK = 128
f32, bf16 = jnp.float32, jnp.bfloat16


def split(x):
    high = x.astype(bf16)
    return high, (x - high.astype(f32)).astype(bf16)


def mm(a, b, bt=False):
    dims = (((1,), (1 if bt else 0,)), ((), ()))
    return lax.dot_general(a, b, dims, preferred_element_type=f32)


def left(x):
    high, low = split(x)
    return jnp.concatenate([high, high, low], axis=1)


def right(x, axis=1):
    high, low = split(x)
    return jnp.concatenate([high, low, high], axis=axis)


def rows_of(x):
    return [jnp.broadcast_to(x[k : k + 1, :], (8, BLK)) for k in range(8)]


def lane(x, j):
    return jnp.broadcast_to(x[:, j : j + 1], (8, BLK))


def recip(x):
    r = pl.reciprocal(x, approx=True)
    return r * (2.0 - x * r)


def tree(terms):
    while len(terms) > 1:
        terms = [sum(terms[i : i + 2][1:], terms[i]) for i in range(0, len(terms), 2)]
    return terms[0]


def factor_inverse(D, store):
    sub = lax.broadcasted_iota(jnp.int32, (8, BLK), 0)
    ln = lax.broadcasted_iota(jnp.int32, (8, BLK), 1)
    E = [jnp.where(sub + 8 * v == ln, 1.0, 0.0).astype(f32) for v in range(16)]
    for g in range(16):
        R, RE = rows_of(D[g]), rows_of(E[g])
        G = {}
        for i in range(8):
            for l in range(i, 8):
                G[i, l] = lane(R[i], 8 * g + l)
        M = {v: [lane(D[v], 8 * g + k) for k in range(8)] for v in range(g + 1, 16)}
        X = list(M[g + 1]) if g < 15 else None
        C, Z, ZE, out = {}, [None] * 8, [None] * 8, None
        for i in range(0, 8, 2):
            p, q, s = G[i, i], G[i, i + 1], G[i + 1, i + 1]
            det = p * s - q * q
            inv = 1.0 / det
            first, last = {}, {}
            for l in range(i + 2, 8):
                first[l] = s * G[i, l] - q * G[i + 1, l]
                last[l] = p * G[i + 1, l] - q * G[i, l]
            for l in range(i + 2, 8):
                for m in range(l, 8):
                    G[l, m] = G[l, m] - (G[i, m] * first[l] + G[i + 1, m] * last[l]) * inv
            pinv, sinv, qinv = p * inv, s * inv, q * inv
            Z[i], Z[i + 1] = sinv * R[i] - qinv * R[i + 1], pinv * R[i + 1] - qinv * R[i]
            ZE[i], ZE[i + 1] = sinv * RE[i] - qinv * RE[i + 1], pinv * RE[i + 1] - qinv * RE[i]
            for l in range(i + 2, 8):
                C[l, i], C[l, i + 1] = first[l] * inv, last[l] * inv
                R[l] = R[l] - (C[l, i] * R[i] + C[l, i + 1] * R[i + 1])
                RE[l] = RE[l] - (C[l, i] * RE[i] + C[l, i + 1] * RE[i + 1])
                if X:
                    X[l] = X[l] - (C[l, i] * X[i] + C[l, i + 1] * X[i + 1])
            ratio = 1.0 / p
            even = RE[i] * lax.rsqrt(p)
            odd = (RE[i + 1] - (q * ratio) * RE[i]) * lax.rsqrt(det * ratio)
            out = even if out is None else jnp.where(sub == i, even, out)
            out = jnp.where(sub == i + 1, odd, out)
        store(g, out)
        if g == 15:
            break
        d = D[g + 1] - tree([X[k] * Z[k] for k in range(6)])
        D[g + 1] = d - (X[6] * Z[6] + X[7] * Z[7])
        E[g + 1] = E[g + 1] - tree([X[k] * ZE[k] for k in range(8)])
        V, VE = [None] * 8, [None] * 8
        for i in range(7, -1, -1):
            low = i + 2 - i % 2
            V[i], VE[i] = Z[i], ZE[i]
            if low < 8:
                V[i] = V[i] - tree([C[l, i] * V[l] for l in range(low, 8)])
                VE[i] = VE[i] - tree([C[l, i] * VE[l] for l in range(low, 8)])
        for v in range(g + 2, 16):
            D[v] = D[v] - tree([M[v][k] * V[k] for k in range(8)])
            E[v] = E[v] - tree([M[v][k] * VE[k] for k in range(8)])


def eliminate(i, t, rt, pa, pb, inverse, solved):
    start = (i + 1) * BLK
    if start == N:
        return
    panel = mm(left(t[start:, i * BLK : start]), inverse, True)
    pa[start:, :] = left(panel)
    pb[start:, :] = right(panel)
    t[start:, start : start + BLK] -= mm(pa[start:, :], pb[start : start + BLK, :], True)


def rest(i, t, rt, pa, pb, solved):
    start = (i + 1) * BLK
    if start == N:
        return
    rt[start:, :] -= mm(pa[start:, :], solved)
    first = start + BLK
    while first < N:
        wide = 256 if (N - first) % 256 == 0 else 128
        t[first:, first : first + wide] -= mm(pa[first:, :], pb[first : first + wide, :], True)
        first += wide


def kernel(c_ref, a_ref, rhs_ref, diag_ref, panel_ref, cand_ref, t, rt, pa, pb, sems):
    copies = []
    for k in range(8):
        rows = pl.ds(k * BLK, BLK)
        edge = N - k * BLK
        pieces = [(0, k * BLK, edge)] + ([(edge, 0, k * BLK)] if k else [])
        for source, target, width in pieces:
            copies.append(
                pltpu.make_async_copy(
                    a_ref.at[rows, pl.ds(source, width)],
                    t.at[rows, pl.ds(target, width)],
                    sems.at[len(copies)],
                )
            )
            copies[-1].start()
    mine = pl.multiple_of(c_ref[0] * 64, 64)
    rt[...] = rhs_ref[...]
    copies[0].wait()
    ri = lax.broadcasted_iota(jnp.int32, (64, BLK), 0) + mine
    ci = lax.broadcasted_iota(jnp.int32, (64, BLK), 1)
    before = None
    for kb in range(8):
        base = kb * BLK
        D = [t[base + 8 * v : base + 8 * v + 8, base : base + BLK] for v in range(16)]
        slabs = []
        factor_inverse(D, lambda g, rows, slabs=slabs: slabs.append(rows))
        if before is not None:
            rest(kb - 1, t, rt, pa.at[(kb - 1) % 2], pb.at[(kb - 1) % 2], before)
        low_inverse = jnp.concatenate(slabs, axis=0)
        if kb == 0:
            for copy in copies[1:]:
                copy.wait()
        inverse = right(low_inverse)
        low = mm(left(t[pl.ds(mine, 64), base : base + BLK]), inverse, True)
        diag_ref[:, base : base + BLK] = jnp.where(ri >= ci + base, low, 0.0)
        solved = mm(left(low_inverse), right(rt[base : base + BLK, :], 0))
        rt[base : base + BLK, :] = solved
        before = right(solved, 0)
        eliminate(kb, t, rt, pa.at[kb % 2], pb.at[kb % 2], inverse, before)
    panel_ref[...] = rt[pl.ds(mine, 64), :64]
    cand_ref[...] = rt[pl.ds(mine, 64), 64:]


def chol_solve(c, a, rhs):
    return pl.pallas_call(
        kernel,
        out_shape=(
            jax.ShapeDtypeStruct((64, N), f32),
            jax.ShapeDtypeStruct((64, 64), f32),
            jax.ShapeDtypeStruct((64, 64), f32),
        ),
        in_specs=[
            pl.BlockSpec(memory_space=pltpu.SMEM),
            pl.BlockSpec(memory_space=pl.ANY),
            pl.BlockSpec(memory_space=pltpu.VMEM),
        ],
        out_specs=(pl.BlockSpec(memory_space=pltpu.VMEM),) * 3,
        scratch_shapes=[
            pltpu.VMEM((N, N), f32),
            pltpu.VMEM((N, BLK), f32),
            pltpu.VMEM((2, N, 3 * BLK), bf16),
            pltpu.VMEM((2, N, 3 * BLK), bf16),
            pltpu.SemaphoreType.DMA((15,)),
        ],
        compiler_params=pltpu.CompilerParams(vmem_limit_bytes=60 * 1024 * 1024),
        cost_estimate=pl.CostEstimate(flops=3 * 10**9, bytes_accessed=5 * 10**6, transcendentals=0),
    )(c, a, rhs)


SMALL = pltpu.CompilerParams(vmem_limit_bytes=8 * 1024 * 1024)


def slab_kernel(c_ref, tiles_ref, out_ref):
    swap = c_ref[0] % 2
    place = lax.broadcasted_iota(jnp.int32, (16, BLK), 1) // 32
    for d in range(8):
        four = []
        for side in range(2):
            for half in range(2):
                four.append(tiles_ref[4 * d + 2 * (side + swap - 2 * side * swap) + half])
        for q in range(4):
            piece = four[0] if q == 0 else pltpu.roll(four[0], BLK - 32 * q, 1)
            for k in range(1, 4):
                turn = (32 * (k - q)) % BLK
                piece = jnp.where(place == k, pltpu.roll(four[k], turn, 1) if turn else four[k], piece)
            out_ref[16 * q : 16 * q + 16, BLK * d : BLK * d + BLK] = piece


def row_slab(c, tiles):
    return pl.pallas_call(
        slab_kernel,
        out_shape=jax.ShapeDtypeStruct((64, N), f32),
        in_specs=[pl.BlockSpec(memory_space=pltpu.SMEM), pl.BlockSpec(memory_space=pltpu.VMEM)],
        out_specs=pl.BlockSpec(memory_space=pltpu.VMEM),
        compiler_params=SMALL,
    )(c, tiles)


def product_kernel(place_ref, packed_ref, out_ref, half_ref):
    distance, side, half = place_ref[0], place_ref[1], place_ref[2]
    lanes = lax.broadcasted_iota(jnp.int32, (16, BLK), 1) // 32
    group = lax.broadcasted_iota(jnp.int32, (80, BLK), 1) // 32
    for r in range(0, 16, 2):
        upper, lower = (
            jnp.concatenate([packed_ref[k, 64:, :].astype(f32), packed_ref[k + 1, 64:, :].astype(f32)], axis=0)
            for k in (r, 16 + r)
        )
        whole = jnp.where(half == 0, upper, pltpu.roll(upper, 96, 1))
        other = jnp.where(half == 0, pltpu.roll(lower, 64, 1), pltpu.roll(lower, 32, 1))
        near = jnp.where(group == 0, whole, pltpu.roll(whole, 96, 1))
        far = jnp.where(group == 2, other, pltpu.roll(other, 96, 1))
        half_ref[40 * r : 40 * r + 80, :] = jnp.where(group < 2, near, far).astype(bf16)
    for c in range(16):
        other = 2 * ((c // 2 + distance) % 8) + (side + c) % 2
        total = None
        for part in range(2):
            at = slice(32 * part, 32 * part + 32)
            left_rows = jnp.concatenate([packed_ref[2 * c, at, :], packed_ref[2 * c + 1, at, :]], axis=0)
            right_rows = packed_ref[2 * other + half, at, :]
            one = mm(left_rows, jnp.concatenate([right_rows] * 4, axis=0), True)
            total = one if total is None else total + one
        piece = total[:16]
        for q in range(1, 4):
            piece = jnp.where(lanes == q, total[16 * q : 16 * q + 16], piece)
        out_ref[c] = piece


def tile_products(place, packed):
    return pl.pallas_call(
        product_kernel,
        out_shape=(
            jax.ShapeDtypeStruct((16, 16, BLK), f32),
            jax.ShapeDtypeStruct((D // 4, BLK), bf16),
        ),
        in_specs=[pl.BlockSpec(memory_space=pltpu.SMEM), pl.BlockSpec(memory_space=pltpu.VMEM)],
        out_specs=(pl.BlockSpec(memory_space=pltpu.VMEM),) * 2,
        compiler_params=SMALL,
    )(place, packed)


def finish_kernel(parts_ref, tile_ref, out_ref):
    total = tree([parts_ref[c] for c in range(16)])
    result = tile_ref[...] - total
    for r in range(32):
        out_ref[r] = result


def finish_tile(parts, tile):
    return pl.pallas_call(
        finish_kernel,
        out_shape=jax.ShapeDtypeStruct((32, 16, BLK), f32),
        in_specs=[pl.BlockSpec(memory_space=pltpu.VMEM), pl.BlockSpec(memory_space=pltpu.VMEM)],
        out_specs=pl.BlockSpec(memory_space=pltpu.VMEM),
        compiler_params=SMALL,
    )(parts, tile)


def spread(value, axis, count):
    copies = jnp.broadcast_to(value[None], (count,) + value.shape)
    return lax.all_to_all(lax.optimization_barrier(copies), axis, 0, 0)


def matern(inner, left_norms, right_norms):
    squared = jnp.maximum(left_norms[:, None] + right_norms[None, :] - 2.0 * inner, 0.0)
    scaled = jnp.sqrt(5.0 * squared / D)
    return (1.0 + scaled + scaled * scaled / 3.0) * jnp.exp(-scaled)


def norms(points):
    return jnp.sum(jnp.square(points.astype(f32)), axis=0)


def times(a, b, dims):
    return lax.dot_general(a, b.astype(bf16), (dims, ((), ())), preferred_element_type=f32)


def body(trail_points, block_points, cand_points, trail_factor, block_factor, cand_solved, noise):
    rows, cols = 32, 16
    row_index = lax.axis_index("row")
    col_index = lax.axis_index("col")
    odd = row_index % 2
    side = row_index // 2 % 2
    distance = row_index // 4
    pad = jnp.zeros((trail_points.shape[1], PAD), bf16)
    points_t = lax.all_gather(
        jnp.concatenate([trail_points.T, cand_points.T, pad], axis=1), "col", axis=0, tiled=True
    )
    block_t = block_points.T
    flat = block_factor.astype(bf16)
    packed = jnp.concatenate(
        [flat[:, :BLK], flat[:, BLK:], jnp.concatenate([block_t[:40], block_t[40:]], axis=1)], axis=0
    )
    packed = spread(packed, "row", rows)
    settle = [((2 * c + h) * cols + c, h * cols + c) for c in range(cols) for h in range(2)]
    own_noise = lax.ppermute(noise, ("row", "col"), settle)
    hop = []
    for r in range(rows):
        for c in range(cols):
            partner = 2 * ((c // 2 + r // 4) % 8) + (r // 2 + c) % 2
            hop.append((r * cols + partner, r * cols + c))
    place = jnp.stack([distance, side, odd]).astype(jnp.int32)
    products, half = tile_products(place, packed)
    partner = lax.ppermute(half, ("row", "col"), hop)
    parts = lax.all_to_all(products, "col", 0, 0)
    own = packed[:, 64:, :].reshape(D // 2, BLK)
    own_norms = norms(own)
    own_norms = own_norms[:64] + own_norms[64:]
    partner_norms = jnp.sum(norms(partner).reshape(4, 32), axis=0)
    ends = (((0,), (0,)), ((), ()))
    near = lax.dot_general(own[: D // 4], partner, ends, preferred_element_type=f32)
    far = lax.dot_general(own[D // 4 :], partner, ends, preferred_element_type=f32)
    inner = (near[:64, :32] + near[64:, 32:64]) + (far[:64, 64:96] + far[64:, 96:])
    tile = matern(inner, own_norms, partner_norms)
    line = jnp.arange(64, dtype=jnp.int32)[:, None] - 32 * odd
    tile = tile + jnp.where(line == jnp.arange(32, dtype=jnp.int32)[None, :], own_noise[None, :], 0.0)
    tile = jnp.concatenate([tile[16 * q : 16 * q + 16] for q in range(4)], axis=1)
    sent = finish_tile(parts, lax.optimization_barrier(tile))
    diag_rows = row_slab(col_index.reshape(1), lax.all_to_all(sent, "row", 0, 0))
    diag_rows, packed = lax.optimization_barrier((diag_rows, packed))
    whole = lax.all_gather(diag_rows, "col", axis=0, tiled=True)

    factor = jnp.concatenate([packed[:, :32], packed[:, 32:64]], axis=2).reshape(N, -1)
    rhs_part = jnp.concatenate(
        [times(factor, trail_factor, ((1,), (1,))), times(factor, cand_solved, ((1,), (0,)))], axis=1
    )
    rhs_parts = lax.all_to_all(rhs_part.astype(bf16).reshape(cols, 64, BLK), "col", 0, 0)
    rhs_sum = jnp.sum(rhs_parts.astype(f32), axis=0)
    points_t = points_t[:, :BLK]
    own_t = jnp.stack([packed[:, 64:, :64], packed[:, 64:, 64:]], axis=1).reshape(D, -1)
    inner = lax.dot_general(own_t, points_t, (((0,), (0,)), ((), ())), preferred_element_type=f32)
    rhs_tile = matern(inner, own_norms, norms(points_t)) - rhs_sum
    rhs = lax.all_gather(rhs_tile, "col", axis=0, tiled=True)
    return chol_solve(col_index.reshape(1).astype(jnp.int32), whole, rhs)


def solution(mesh):
    return jax.shard_map(
        body,
        mesh=mesh,
        in_specs=(
            P("row", "col"),
            P("col", "row"),
            P("row", "col"),
            P("row", "col"),
            P("row", "col"),
            P("col", "row"),
            P("row"),
        ),
        out_specs=(P("col", None), P("col", "row"), P("col", "row")),
        check_vma=False,
    )
```

```python
import jax
import jax.numpy as jnp
from jax import lax
from jax.experimental import pallas as pl
from jax.experimental.pallas import tpu as pltpu
from jax.sharding import PartitionSpec as P

D = 2560
PAD = 128

N = 1024
BLK = 128
f32, bf16 = jnp.float32, jnp.bfloat16


def split(x):
    high = x.astype(bf16)
    return high, (x - high.astype(f32)).astype(bf16)


def mm(a, b, bt=False):
    dims = (((1,), (1 if bt else 0,)), ((), ()))
    return lax.dot_general(a, b, dims, preferred_element_type=f32)


def left(x):
    high, low = split(x)
    return jnp.concatenate([high, high, low], axis=1)


def right(x, axis=1):
    high, low = split(x)
    return jnp.concatenate([high, low, high], axis=axis)


def rows_of(x):
    return [jnp.broadcast_to(x[k : k + 1, :], (8, BLK)) for k in range(8)]


def lane(x, j):
    return jnp.broadcast_to(x[:, j : j + 1], (8, BLK))


def recip(x):
    r = pl.reciprocal(x, approx=True)
    return r * (2.0 - x * r)


def tree(terms):
    while len(terms) > 1:
        terms = [sum(terms[i : i + 2][1:], terms[i]) for i in range(0, len(terms), 2)]
    return terms[0]


def factor_inverse(D, store):
    sub = lax.broadcasted_iota(jnp.int32, (8, BLK), 0)
    ln = lax.broadcasted_iota(jnp.int32, (8, BLK), 1)
    E = [jnp.where(sub + 8 * v == ln, 1.0, 0.0).astype(f32) for v in range(16)]
    for g in range(16):
        R, RE = rows_of(D[g]), rows_of(E[g])
        G = {}
        for i in range(8):
            for l in range(i, 8):
                G[i, l] = lane(R[i], 8 * g + l)
        M = {v: [lane(D[v], 8 * g + k) for k in range(8)] for v in range(g + 1, 16)}
        X = list(M[g + 1]) if g < 15 else None
        C, Z, ZE, out = {}, [None] * 8, [None] * 8, None
        for i in range(0, 8, 2):
            p, q, s = G[i, i], G[i, i + 1], G[i + 1, i + 1]
            det = p * s - q * q
            inv = 1.0 / det
            first, last = {}, {}
            for l in range(i + 2, 8):
                first[l] = s * G[i, l] - q * G[i + 1, l]
                last[l] = p * G[i + 1, l] - q * G[i, l]
            for l in range(i + 2, 8):
                for m in range(l, 8):
                    G[l, m] = G[l, m] - (G[i, m] * first[l] + G[i + 1, m] * last[l]) * inv
            pinv, sinv, qinv = p * inv, s * inv, q * inv
            Z[i], Z[i + 1] = sinv * R[i] - qinv * R[i + 1], pinv * R[i + 1] - qinv * R[i]
            ZE[i], ZE[i + 1] = sinv * RE[i] - qinv * RE[i + 1], pinv * RE[i + 1] - qinv * RE[i]
            for l in range(i + 2, 8):
                C[l, i], C[l, i + 1] = first[l] * inv, last[l] * inv
                R[l] = R[l] - (C[l, i] * R[i] + C[l, i + 1] * R[i + 1])
                RE[l] = RE[l] - (C[l, i] * RE[i] + C[l, i + 1] * RE[i + 1])
                if X:
                    X[l] = X[l] - (C[l, i] * X[i] + C[l, i + 1] * X[i + 1])
            ratio = 1.0 / p
            even = RE[i] * lax.rsqrt(p)
            odd = (RE[i + 1] - (q * ratio) * RE[i]) * lax.rsqrt(det * ratio)
            out = even if out is None else jnp.where(sub == i, even, out)
            out = jnp.where(sub == i + 1, odd, out)
        store(g, out)
        if g == 15:
            break
        d = D[g + 1] - tree([X[k] * Z[k] for k in range(6)])
        D[g + 1] = d - (X[6] * Z[6] + X[7] * Z[7])
        E[g + 1] = E[g + 1] - tree([X[k] * ZE[k] for k in range(8)])
        V, VE = [None] * 8, [None] * 8
        for i in range(7, -1, -1):
            low = i + 2 - i % 2
            V[i], VE[i] = Z[i], ZE[i]
            if low < 8:
                V[i] = V[i] - tree([C[l, i] * V[l] for l in range(low, 8)])
                VE[i] = VE[i] - tree([C[l, i] * VE[l] for l in range(low, 8)])
        for v in range(g + 2, 16):
            D[v] = D[v] - tree([M[v][k] * V[k] for k in range(8)])
            E[v] = E[v] - tree([M[v][k] * VE[k] for k in range(8)])


def eliminate(i, t, rt, pa, pb, inverse, solved):
    start = (i + 1) * BLK
    if start == N:
        return
    panel = mm(left(t[start:, i * BLK : start]), inverse, True)
    pa[start:, :] = left(panel)
    pb[start:, :] = right(panel)
    t[start:, start : start + BLK] -= mm(pa[start:, :], pb[start : start + BLK, :], True)


def rest(i, t, rt, pa, pb, solved):
    start = (i + 1) * BLK
    if start == N:
        return
    rt[start:, :] -= mm(pa[start:, :], solved)
    first = start + BLK
    while first < N:
        wide = 256 if (N - first) % 256 == 0 else 128
        t[first:, first : first + wide] -= mm(pa[first:, :], pb[first : first + wide, :], True)
        first += wide


def kernel(c_ref, a_ref, rhs_ref, diag_ref, panel_ref, cand_ref, t, rt, pa, pb, sems):
    copies = []
    for k in range(8):
        rows = pl.ds(k * BLK, BLK)
        edge = N - k * BLK
        pieces = [(0, k * BLK, edge)] + ([(edge, 0, k * BLK)] if k else [])
        for source, target, width in pieces:
            copies.append(
                pltpu.make_async_copy(
                    a_ref.at[rows, pl.ds(source, width)],
                    t.at[rows, pl.ds(target, width)],
                    sems.at[len(copies)],
                )
            )
            copies[-1].start()
    mine = pl.multiple_of(c_ref[0] * 64, 64)
    rt[...] = rhs_ref[...]
    copies[0].wait()
    ri = lax.broadcasted_iota(jnp.int32, (64, BLK), 0) + mine
    ci = lax.broadcasted_iota(jnp.int32, (64, BLK), 1)
    before = None
    for kb in range(8):
        base = kb * BLK
        D = [t[base + 8 * v : base + 8 * v + 8, base : base + BLK] for v in range(16)]
        slabs = []
        factor_inverse(D, lambda g, rows, slabs=slabs: slabs.append(rows))
        if before is not None:
            rest(kb - 1, t, rt, pa.at[(kb - 1) % 2], pb.at[(kb - 1) % 2], before)
        low_inverse = jnp.concatenate(slabs, axis=0)
        if kb == 0:
            for copy in copies[1:]:
                copy.wait()
        inverse = right(low_inverse)
        low = mm(left(t[pl.ds(mine, 64), base : base + BLK]), inverse, True)
        diag_ref[:, base : base + BLK] = jnp.where(ri >= ci + base, low, 0.0)
        solved = mm(left(low_inverse), right(rt[base : base + BLK, :], 0))
        rt[base : base + BLK, :] = solved
        before = right(solved, 0)
        eliminate(kb, t, rt, pa.at[kb % 2], pb.at[kb % 2], inverse, before)
    panel_ref[...] = rt[pl.ds(mine, 64), :64]
    cand_ref[...] = rt[pl.ds(mine, 64), 64:]


def chol_solve(c, a, rhs):
    return pl.pallas_call(
        kernel,
        out_shape=(
            jax.ShapeDtypeStruct((64, N), f32),
            jax.ShapeDtypeStruct((64, 64), f32),
            jax.ShapeDtypeStruct((64, 64), f32),
        ),
        in_specs=[
            pl.BlockSpec(memory_space=pltpu.SMEM),
            pl.BlockSpec(memory_space=pl.ANY),
            pl.BlockSpec(memory_space=pltpu.VMEM),
        ],
        out_specs=(pl.BlockSpec(memory_space=pltpu.VMEM),) * 3,
        scratch_shapes=[
            pltpu.VMEM((N, N), f32),
            pltpu.VMEM((N, BLK), f32),
            pltpu.VMEM((2, N, 3 * BLK), bf16),
            pltpu.VMEM((2, N, 3 * BLK), bf16),
            pltpu.SemaphoreType.DMA((15,)),
        ],
        compiler_params=pltpu.CompilerParams(vmem_limit_bytes=60 * 1024 * 1024),
        cost_estimate=pl.CostEstimate(flops=3 * 10**9, bytes_accessed=5 * 10**6, transcendentals=0),
    )(c, a, rhs)


SMALL = pltpu.CompilerParams(vmem_limit_bytes=8 * 1024 * 1024)


def pack_kernel(factor_ref, points_ref, out_ref):
    factor = factor_ref[...].astype(bf16)
    points = points_ref[...].astype(f32).T
    points = jnp.concatenate([points[:40], points[40:]], axis=1).astype(bf16)
    for r in range(32):
        out_ref[r, :32, :] = factor[:, :BLK]
        out_ref[r, 32:64, :] = factor[:, BLK:]
        out_ref[r, 64:, :] = points


def pack_copies(factor, points):
    return pl.pallas_call(
        pack_kernel,
        out_shape=jax.ShapeDtypeStruct((32, 104, BLK), bf16),
        in_specs=[pl.BlockSpec(memory_space=pltpu.VMEM)] * 2,
        out_specs=pl.BlockSpec(memory_space=pltpu.VMEM),
        compiler_params=SMALL,
    )(factor, points)


def slab_kernel(c_ref, tiles_ref, out_ref):
    swap = c_ref[0] % 2
    place = lax.broadcasted_iota(jnp.int32, (16, BLK), 1) // 32
    for d in range(8):
        four = []
        for side in range(2):
            for half in range(2):
                four.append(tiles_ref[4 * d + 2 * (side + swap - 2 * side * swap) + half])
        for q in range(4):
            piece = four[0] if q == 0 else pltpu.roll(four[0], BLK - 32 * q, 1)
            for k in range(1, 4):
                turn = (32 * (k - q)) % BLK
                piece = jnp.where(place == k, pltpu.roll(four[k], turn, 1) if turn else four[k], piece)
            out_ref[16 * q : 16 * q + 16, BLK * d : BLK * d + BLK] = piece


def row_slab(c, tiles):
    return pl.pallas_call(
        slab_kernel,
        out_shape=jax.ShapeDtypeStruct((64, N), f32),
        in_specs=[pl.BlockSpec(memory_space=pltpu.SMEM), pl.BlockSpec(memory_space=pltpu.VMEM)],
        out_specs=pl.BlockSpec(memory_space=pltpu.VMEM),
        compiler_params=SMALL,
    )(c, tiles)


def product_kernel(place_ref, packed_ref, out_ref, half_ref):
    distance, side, half = place_ref[0], place_ref[1], place_ref[2]
    lanes = lax.broadcasted_iota(jnp.int32, (16, BLK), 1) // 32
    group = lax.broadcasted_iota(jnp.int32, (80, BLK), 1) // 32
    for r in range(0, 16, 2):
        upper, lower = (
            jnp.concatenate([packed_ref[k, 64:, :].astype(f32), packed_ref[k + 1, 64:, :].astype(f32)], axis=0)
            for k in (r, 16 + r)
        )
        whole = jnp.where(half == 0, upper, pltpu.roll(upper, 96, 1))
        other = jnp.where(half == 0, pltpu.roll(lower, 64, 1), pltpu.roll(lower, 32, 1))
        near = jnp.where(group == 0, whole, pltpu.roll(whole, 96, 1))
        far = jnp.where(group == 2, other, pltpu.roll(other, 96, 1))
        half_ref[40 * r : 40 * r + 80, :] = jnp.where(group < 2, near, far).astype(bf16)
    for c in range(16):
        other = 2 * ((c // 2 + distance) % 8) + (side + c) % 2
        total = None
        for part in range(2):
            at = slice(32 * part, 32 * part + 32)
            left_rows = jnp.concatenate([packed_ref[2 * c, at, :], packed_ref[2 * c + 1, at, :]], axis=0)
            right_rows = packed_ref[2 * other + half, at, :]
            one = mm(left_rows, jnp.concatenate([right_rows] * 4, axis=0), True)
            total = one if total is None else total + one
        piece = total[:16]
        for q in range(1, 4):
            piece = jnp.where(lanes == q, total[16 * q : 16 * q + 16], piece)
        out_ref[c] = piece


def tile_products(place, packed):
    return pl.pallas_call(
        product_kernel,
        out_shape=(
            jax.ShapeDtypeStruct((16, 16, BLK), f32),
            jax.ShapeDtypeStruct((D // 4, BLK), bf16),
        ),
        in_specs=[pl.BlockSpec(memory_space=pltpu.SMEM), pl.BlockSpec(memory_space=pltpu.VMEM)],
        out_specs=(pl.BlockSpec(memory_space=pltpu.VMEM),) * 2,
        compiler_params=SMALL,
    )(place, packed)


def finish_kernel(parts_ref, tile_ref, out_ref):
    total = tree([parts_ref[c] for c in range(16)])
    result = tile_ref[...] - total
    for r in range(32):
        out_ref[r] = result


def finish_tile(parts, tile):
    return pl.pallas_call(
        finish_kernel,
        out_shape=jax.ShapeDtypeStruct((32, 16, BLK), f32),
        in_specs=[pl.BlockSpec(memory_space=pltpu.VMEM), pl.BlockSpec(memory_space=pltpu.VMEM)],
        out_specs=pl.BlockSpec(memory_space=pltpu.VMEM),
        compiler_params=SMALL,
    )(parts, tile)


def matern(inner, left_norms, right_norms):
    squared = jnp.maximum(left_norms[:, None] + right_norms[None, :] - 2.0 * inner, 0.0)
    scaled = jnp.sqrt(5.0 * squared / D)
    return (1.0 + scaled + scaled * scaled / 3.0) * jnp.exp(-scaled)


def norms(points):
    return jnp.sum(jnp.square(points.astype(f32)), axis=0)


def times(a, b, dims):
    return lax.dot_general(a, b.astype(bf16), (dims, ((), ())), preferred_element_type=f32)


def body(trail_points, block_points, cand_points, trail_factor, block_factor, cand_solved, noise):
    rows, cols = 32, 16
    row_index = lax.axis_index("row")
    col_index = lax.axis_index("col")
    odd = row_index % 2
    side = row_index // 2 % 2
    distance = row_index // 4
    pad = jnp.zeros((trail_points.shape[1], PAD), bf16)
    points_t = lax.all_gather(
        jnp.concatenate([trail_points.T, cand_points.T, pad], axis=1), "col", axis=0, tiled=True
    )
    packed = lax.all_to_all(pack_copies(block_factor, block_points), "row", 0, 0)
    settle = [((2 * c + h) * cols + c, h * cols + c) for c in range(cols) for h in range(2)]
    own_noise = lax.ppermute(noise, ("row", "col"), settle)
    hop = []
    for r in range(rows):
        for c in range(cols):
            partner = 2 * ((c // 2 + r // 4) % 8) + (r // 2 + c) % 2
            hop.append((r * cols + partner, r * cols + c))
    place = jnp.stack([distance, side, odd]).astype(jnp.int32)
    products, half = tile_products(place, packed)
    partner = lax.ppermute(half, ("row", "col"), hop)
    parts = lax.all_to_all(products, "col", 0, 0)
    own = packed[:, 64:, :].reshape(D // 2, BLK)
    own_norms = norms(own)
    own_norms = own_norms[:64] + own_norms[64:]
    partner_norms = jnp.sum(norms(partner).reshape(4, 32), axis=0)
    ends = (((0,), (0,)), ((), ()))
    near = lax.dot_general(own[: D // 4], partner, ends, preferred_element_type=f32)
    far = lax.dot_general(own[D // 4 :], partner, ends, preferred_element_type=f32)
    inner = (near[:64, :32] + near[64:, 32:64]) + (far[:64, 64:96] + far[64:, 96:])
    tile = matern(inner, own_norms, partner_norms)
    line = jnp.arange(64, dtype=jnp.int32)[:, None] - 32 * odd
    tile = tile + jnp.where(line == jnp.arange(32, dtype=jnp.int32)[None, :], own_noise[None, :], 0.0)
    tile = jnp.concatenate([tile[16 * q : 16 * q + 16] for q in range(4)], axis=1)
    sent = finish_tile(parts, lax.optimization_barrier(tile))
    diag_rows = row_slab(col_index.reshape(1), lax.all_to_all(sent, "row", 0, 0))
    diag_rows, packed = lax.optimization_barrier((diag_rows, packed))
    whole = lax.all_gather(diag_rows, "col", axis=0, tiled=True)

    factor = jnp.concatenate([packed[:, :32], packed[:, 32:64]], axis=2).reshape(N, -1)
    rhs_part = jnp.concatenate(
        [times(factor, trail_factor, ((1,), (1,))), times(factor, cand_solved, ((1,), (0,)))], axis=1
    )
    rhs_parts = lax.all_to_all(rhs_part.astype(bf16).reshape(cols, 64, BLK), "col", 0, 0)
    rhs_sum = jnp.sum(rhs_parts.astype(f32), axis=0)
    points_t = points_t[:, :BLK]
    own_t = jnp.stack([packed[:, 64:, :64], packed[:, 64:, 64:]], axis=1).reshape(D, -1)
    inner = lax.dot_general(own_t, points_t, (((0,), (0,)), ((), ())), preferred_element_type=f32)
    rhs_tile = matern(inner, own_norms, norms(points_t)) - rhs_sum
    rhs = lax.all_gather(rhs_tile, "col", axis=0, tiled=True)
    return chol_solve(col_index.reshape(1).astype(jnp.int32), whole, rhs)


def solution(mesh):
    return jax.shard_map(
        body,
        mesh=mesh,
        in_specs=(
            P("row", "col"),
            P("col", "row"),
            P("row", "col"),
            P("row", "col"),
            P("row", "col"),
            P("col", "row"),
            P("row"),
        ),
        out_specs=(P("col", None), P("col", "row"), P("col", "row")),
        check_vma=False,
    )
```
